256 devices in a mesh: group: 4 (over x), session: 64 (over z, y, core).
Axes of the slice: x: 4, y: 4, z: 8, core: 2. Of those that a mesh axis runs over, the one named last changes fastest.
Arguments:
- spikes: bfloat16 [98304, 128], P(('group', 'session')), may hold values from -6 to 6
- row_owner: int32 [98304, 1], P(('group', 'session')), may hold values from 0 to 63; in each aligned block of 384 rows (0 to 383, 384 to 767, ...) at most 12 rows name the same one
- row_block: int32 [98304], P(('group', 'session')), may hold values from 0 to 1
- chan_count: int32 [128], P('session'), may hold values from 96 to 128
- readin: bfloat16 [16384, 1024], P('session'), may hold values from -0.5 to 0.5
- readout: bfloat16 [1024, 16384], P(None, 'session'), may hold values from -0.1875 to 0.1875
- first_layer: bfloat16 [1024, 1024], replicated, may hold values from -0.1875 to 0.1875
- second_layer: bfloat16 [1024, 1024], replicated, may hold values from -0.1875 to 0.1875
Outputs:
- rebuilt: bfloat16 [98304, 128], P(('group', 'session'))
- readin_grad: float32 [16384, 1024], P('session')
- readout_grad: float32 [1024, 16384], P(None, 'session')
- first_grad: float32 [1024, 1024], P('session')
- second_grad: float32 [1024, 1024], P('session')
The draws below stay inside these ranges and needn't reach their ends.
Inputs may be any that keep to these rules, and one draw needn't show every extreme that they name: `row_owner`: among the 384 rows of one device, no owner is named by more than 12 rows, a bound that some block reaches.
All inputs are finite; a program needn't handle non-finite values.
Results may differ from the reference program's by a relative error of at most 0.012.
Values may be sent and summed in bfloat16 or wider, within the bound.
No kernel may reach another device: no remote copies, remote signals or barrier semaphores. Data moves between devices by JAX's collectives and lax.ppermute only.
A program may use at most 64 MiB of HBM per device.

```python
import math
import jax
import jax.numpy as jnp
import numpy as np
from jax import lax

CH = 128
LAT = 1024
HID = 1024
BLK_DEV = 2
ROWS_DEV = 384
CAP = 12
NB = 128
ROWS = 98304
N_GROUP = 4
N_SESSION = 64


def with_ends(result, stream_key, least, largest):
    shape = result.shape
    spot = [jax.random.randint(jax.random.fold_in(stream_key, axis), (), 0, shape[axis]) for axis in range(len(shape))]
    result = result.at[tuple(spot)].set(least)
    longest = shape.index(max(shape))
    spot[longest] = (spot[longest] + 1) % shape[longest]
    return result.at[tuple(spot)].set(largest)


def level_of(own_key, extent, pieces, low, high):
    factor_of, own = 1.0, jax.random.fold_in(own_key, 6)
    for dim, blocks in pieces:
        draws = jnp.exp(jax.random.uniform(jax.random.fold_in(own, dim), (blocks,), jnp.float32, low / len(pieces), high / len(pieces)))
        factor_of = factor_of * jnp.repeat(draws, extent[dim] // blocks).reshape([-1 if axis == dim else 1 for axis in range(len(extent))])
    return factor_of


def assign_block(stream_key, own, number, rows, amount, top, reach, lean):
    sequence = jax.random.permutation(stream_key, amount)
    packed, usual = load_shares(amount, rows * top, reach, lean, True), load_shares(amount, rows * top, reach, lean, False)
    places = jnp.arange(amount)

    def named(tallies, offset_by):
        used = int((tallies > 0).sum())
        fixed = max(1, used // 4)
        shifted = fixed + (places - fixed + offset_by * (used - fixed)) % max(1, amount - fixed)
        return jnp.zeros((amount,), jnp.int32).at[sequence[jnp.where(places < fixed, places, shifted)]].set(jnp.asarray(tallies, jnp.int32))

    tallies = jnp.where(number % 4 == 0, named(packed, number // 4), named(usual, number - number // 4 - 1))
    mixed = jax.random.permutation(jax.random.fold_in(own, 3), amount)
    giver, sink = mixed[0:amount // 2 * 2:2], mixed[1:amount // 2 * 2:2]
    slack = jnp.minimum(tallies[giver] - 1, reach - tallies[sink]) // 2
    slack = jnp.where((giver == sequence[0]) | (sink == sequence[0]) | (tallies[sink] == 0), 0, jnp.maximum(slack, 0))
    shifted = jax.random.randint(jax.random.fold_in(own, 4), (amount // 2,), 0, 1 << 20) % (slack + 1)
    tallies = tallies.at[giver].add(-shifted).at[sink].add(shifted)
    members = jnp.searchsorted(jnp.cumsum(tallies), jnp.arange(rows * top), side="right").astype(jnp.int32)
    table = members.reshape(top, rows).T
    table = table[jax.random.permutation(jax.random.fold_in(own, 1), rows)]
    offset_by = jax.random.randint(jax.random.fold_in(own, 2), (rows, 1), 0, top)
    return jnp.take_along_axis(table, (jnp.arange(top)[None, :] + offset_by) % top, axis=1)


def load_shares(number_of, total, bound, skew, full):
    portions = [(1 << 20) // math.isqrt(grade ** skew) + 1 for grade in range(1, number_of + 1)]
    largest = bound if full else min(bound, max(-(-total // number_of), total * portions[0] // sum(portions)))
    least = 1 if total - largest >= number_of - 1 else 0
    given, spare = [largest] + [least] * (number_of - 1), total - largest - least * (number_of - 1)
    while spare > 0:
        movable = [i for i in range(1, number_of) if given[i] < largest] or [i for i in range(1, number_of) if given[i] < bound]
        whole, remaining = sum([portions[i] for i in movable]), spare
        for i in movable:
            extra = min(bound - given[i], max(1, remaining * portions[i] // whole), spare)
            given[i] = given[i] + extra
            spare = spare - extra
    return np.array(given)


def centred(stream_key, shape, scale, most, cuts=(), held_as=jnp.bfloat16):
    drawn = jax.random.normal(stream_key, shape, jnp.float32) * scale
    if len(cuts) > 0:
        drawn = level_of(stream_key, shape, cuts, -0.22, 0.18) * drawn
    return jnp.clip(drawn, min=-most, max=most).astype(held_as)


def setup_inputs(seed: int = 0) -> dict:
    arg_keys = jax.random.split(jax.random.key(seed), 9)
    spikes = centred(arg_keys[0], (ROWS, CH), 1.0, 6.0, ((0, 256),))
    row_owner_keys = jax.random.split(jax.random.fold_in(arg_keys[1], 1), ROWS // ROWS_DEV)
    row_owner_turns = jax.random.permutation(jax.random.fold_in(arg_keys[1], 3), ROWS // ROWS_DEV)
    row_owner = jax.vmap(lambda own, number: assign_block(jax.random.fold_in(arg_keys[1], 2), own, number, ROWS_DEV, N_SESSION, 1, CAP, 2))(row_owner_keys, row_owner_turns).reshape((ROWS, 1))
    row_block = with_ends(jax.random.randint(arg_keys[2], (ROWS,), 0, BLK_DEV), jax.random.fold_in(arg_keys[2], 1), 0, BLK_DEV - 1).astype(jnp.int32)
    chan_count = with_ends(jax.random.randint(arg_keys[3], (NB,), 3 * CH // 4, CH + 1), jax.random.fold_in(arg_keys[3], 1), 3 * CH // 4, CH).astype(jnp.int32)
    readin = centred(arg_keys[4], (NB * CH, LAT), CH ** -0.5, 0.5, ((0, 64),))
    readout = centred(arg_keys[5], (LAT, NB * CH), LAT ** -0.5, 0.1875, ((1, 64),))
    first_layer = centred(arg_keys[6], (LAT, HID), LAT ** -0.5, 0.1875)
    second_layer = centred(arg_keys[7], (HID, LAT), HID ** -0.5, 0.1875)
    return dict(spikes=spikes, row_owner=row_owner, row_block=row_block, chan_count=chan_count, readin=readin, readout=readout, first_layer=first_layer, second_layer=second_layer)


def owner_pass(spike_rows, owner_rows, block_rows, owner_at, chan_count, readin, readout, first_layer, second_layer):
    slot_count = 2 * ROWS_DEV
    order = jnp.argsort((owner_rows != owner_at).astype(jnp.int32), stable=True)[:slot_count].astype(jnp.int32)
    valid = owner_rows[order] == owner_at
    taken = spike_rows[order]
    labels = block_rows[order]
    counts_here = lax.dynamic_slice_in_dim(chan_count, owner_at * BLK_DEV, BLK_DEV)
    w_in = lax.dynamic_slice_in_dim(readin, owner_at * BLK_DEV * CH, BLK_DEV * CH, 0)
    w_out = lax.dynamic_slice_in_dim(readout, owner_at * BLK_DEV * CH, BLK_DEV * CH, 1)
    chosen = (labels[:, None] == jnp.arange(BLK_DEV, dtype=jnp.int32)[None, :]) & valid[:, None]
    counts = jnp.sum(jnp.where(chosen, counts_here[None, :], 0), axis=1)
    visible = jnp.arange(CH, dtype=jnp.int32)[None, :] < counts[:, None]
    inputs = jnp.where(visible, taken, jnp.zeros_like(taken))
    chosen_b = chosen.astype(inputs.dtype)
    spread = (chosen_b[:, :, None] * inputs[:, None, :]).reshape(slot_count, BLK_DEV * CH)
    factors = jnp.dot(spread, w_in, preferred_element_type=jnp.float32).astype(jnp.bfloat16)
    pre_act = jnp.dot(factors, first_layer, preferred_element_type=jnp.float32)
    activity = jax.nn.silu(pre_act).astype(jnp.bfloat16)
    latent = jnp.dot(activity, second_layer, preferred_element_type=jnp.float32).astype(jnp.bfloat16)
    wide_rates = jnp.dot(latent, w_out, preferred_element_type=jnp.float32)
    rates = jnp.sum(chosen.astype(jnp.float32)[:, :, None] * wide_rates.reshape(slot_count, BLK_DEV, CH), axis=1)
    rebuilt_slots = jnp.where(visible, rates, 0.0).astype(jnp.bfloat16)
    weight = (BLK_DEV / ROWS_DEV) ** 0.5
    errors = (jnp.where(visible, rates - inputs.astype(jnp.float32), 0.0) * weight).astype(jnp.bfloat16)
    err_wide = (chosen_b[:, :, None] * errors[:, None, :]).reshape(slot_count, BLK_DEV * CH)
    dims_rows = (((0,), (0,)), ((), ()))
    dims_cols = (((1,), (1,)), ((), ()))
    grad_out = lax.dot_general(latent, err_wide, dims_rows, preferred_element_type=jnp.float32)
    d_latent = lax.dot_general(err_wide, w_out, dims_cols, preferred_element_type=jnp.float32).astype(jnp.bfloat16)
    grad_two = lax.dot_general(activity, d_latent, dims_rows, preferred_element_type=jnp.float32)
    d_act = lax.dot_general(d_latent, second_layer, dims_cols, preferred_element_type=jnp.float32)
    sigmoid_pre = jax.nn.sigmoid(pre_act)
    d_pre = (d_act * sigmoid_pre * (1.0 + pre_act * (1.0 - sigmoid_pre))).astype(jnp.bfloat16)
    grad_one = lax.dot_general(factors, d_pre, dims_rows, preferred_element_type=jnp.float32)
    d_factors = lax.dot_general(d_pre, first_layer, dims_cols, preferred_element_type=jnp.float32).astype(jnp.bfloat16)
    grad_in = lax.dot_general(spread, d_factors, dims_rows, preferred_element_type=jnp.float32)
    return rebuilt_slots, order, grad_in, grad_out, grad_one, grad_two


def reference(spikes, row_owner, row_block, chan_count, readin, readout, first_layer, second_layer):
    group_rows = N_SESSION * ROWS_DEV
    spike_all = spikes.reshape(N_GROUP, group_rows, CH)
    owner_all = row_owner.reshape(N_GROUP, group_rows)
    block_all = row_block.reshape(N_GROUP, group_rows)

    def step(carry, index_pair):
        rebuilt, grad_in, grad_out, grad_one, grad_two = carry
        group_at = index_pair // N_SESSION
        owner_at = index_pair % N_SESSION
        spike_rows = lax.dynamic_index_in_dim(spike_all, group_at, 0, keepdims=False)
        owner_rows = lax.dynamic_index_in_dim(owner_all, group_at, 0, keepdims=False)
        block_rows = lax.dynamic_index_in_dim(block_all, group_at, 0, keepdims=False)
        slots, order, part_in, part_out, part_one, part_two = owner_pass(
            spike_rows, owner_rows, block_rows, owner_at, chan_count, readin, readout, first_layer, second_layer)
        rebuilt_group = lax.dynamic_index_in_dim(rebuilt, group_at, 0, keepdims=False)
        rebuilt_group = rebuilt_group.at[order].add(slots)
        rebuilt = lax.dynamic_update_index_in_dim(rebuilt, rebuilt_group, group_at, 0)
        start = owner_at * BLK_DEV * CH
        old_in = lax.dynamic_slice_in_dim(grad_in, start, BLK_DEV * CH, 0)
        grad_in = lax.dynamic_update_slice_in_dim(grad_in, old_in + part_in, start, 0)
        old_out = lax.dynamic_slice_in_dim(grad_out, start, BLK_DEV * CH, 1)
        grad_out = lax.dynamic_update_slice_in_dim(grad_out, old_out + part_out, start, 1)
        return (rebuilt, grad_in, grad_out, grad_one + part_one, grad_two + part_two), None

    start_carry = (jnp.zeros((N_GROUP, group_rows, CH), jnp.bfloat16),
                   jnp.zeros((NB * CH, LAT), jnp.float32),
                   jnp.zeros((LAT, NB * CH), jnp.float32),
                   jnp.zeros((LAT, HID), jnp.float32),
                   jnp.zeros((HID, LAT), jnp.float32))
    pairs = jnp.arange(N_GROUP * N_SESSION, dtype=jnp.int32)
    final, unused = lax.scan(step, start_carry, pairs)
    rebuilt, grad_in, grad_out, grad_one, grad_two = final
    grad_scale = 1.0 / (NB ** 0.5)
    return rebuilt.reshape(ROWS, CH), grad_in, grad_out, grad_one * grad_scale, grad_two * grad_scale
```

```python
import functools

import jax
import jax.numpy as jnp
from jax import lax
from jax.experimental import pallas as pl
from jax.experimental.pallas import tpu as pltpu
from jax.sharding import Mesh, PartitionSpec as P

ZS, YS, CS = 8, 4, 2
CH = 128
STRIDE = 16
CAP = 12
TILE = 256
BF = jnp.bfloat16
F32 = jnp.float32
ROWS_DIMS = (((0,), (0,)), ((), ()))
COLS_DIMS = (((1,), (1,)), ((), ()))


def dot(a, b):
    return jnp.dot(a, b, preferred_element_type=F32)


def dot_rows(a, b):
    return lax.dot_general(a, b, ROWS_DIMS, preferred_element_type=F32)


def dot_cols(a, b):
    return lax.dot_general(a, b, COLS_DIMS, preferred_element_type=F32)


def iota(shape, dim):
    return lax.broadcasted_iota(jnp.int32, shape, dim)


def pack_kernel(owner_ref, block_ref, spikes_ref, packed_ref, target_ref):
    rows = spikes_ref.shape[0]
    slots = packed_ref.shape[0]
    owner = owner_ref[...]
    match = owner == iota((rows, CH), 1)
    earlier = (iota((rows, rows), 1) < iota((rows, rows), 0)).astype(BF)
    before = dot(earlier, match.astype(F32).astype(BF))
    rank = jnp.sum(jnp.where(match, before, 0.0), axis=1, keepdims=True).astype(jnp.int32)
    target = owner * STRIDE + rank
    target_ref[...] = target
    label = (block_ref[...] + 1).astype(F32)
    label_rows = jnp.where(iota((rows, CH), 1) == rank, label, 0.0).astype(BF)
    slot_ids = iota((rows, slots), 1)
    place = (slot_ids == target).astype(F32).astype(BF)
    label_place = (slot_ids == owner * STRIDE + CAP).astype(F32).astype(BF)
    packed_ref[...] = (dot_rows(place, spikes_ref[...]) + dot_rows(label_place, label_rows)).astype(BF)


def unpack_kernel(target_ref, back_ref, rebuilt_ref):
    rows = rebuilt_ref.shape[0]
    slots = back_ref.shape[0]
    place = (iota((rows, slots), 1) == target_ref[...]).astype(F32).astype(BF)
    rebuilt_ref[...] = dot(place, back_ref[...]).astype(BF)


def split_pair(core, tile, send_ref, own_ref, at):
    cols = tile.shape[1]
    first = core == 0
    for j in range(8):
        low, high = tile[32 * j : 32 * j + 16], tile[32 * j + 16 : 32 * j + 32]
        z, y = at * 2 + j // 4, j % 4
        send_ref[y, z] = jnp.where(first, high, low).astype(BF)
        own_ref[y, z] = jnp.where(first, low, high).astype(BF)


def forward_kernel(weight, core_ref, count_ref, got_ref, win_ref, wout_ref, one_ref, two_ref,
                   slots_ref, gout_ref, spread_ref, factors_ref, pre_ref, dlat_ref, send_ref, own_ref,
                   act_ref, lat_ref, err_ref, lab_ref, reb_ref):
    rows = spread_ref.shape[0]
    per, wide = 16 * CAP, 16 * STRIDE
    row, col = iota((per, wide), 0), iota((per, wide), 1)
    source = (row * 5462) >> 16
    pick = (col == source * STRIDE + row - source * CAP).astype(F32).astype(BF)
    pick_label = (col == source * STRIDE + CAP).astype(F32).astype(BF)
    row1, lane = iota((per, CH), 0), iota((per, CH), 1)
    rank1 = row1 - ((row1 * 5462) >> 16) * CAP
    for b in range(rows // per):
        block = got_ref[b * wide : (b + 1) * wide]
        taken = dot(pick, block)
        label = jnp.sum(jnp.where(lane == rank1, dot(pick_label, block), 0.0), axis=1, keepdims=True)
        counts = jnp.where(label == 1.0, count_ref[0], jnp.where(label == 2.0, count_ref[1], 0))
        inputs = jnp.where(lane < counts, taken, 0.0)
        here = pl.ds(b * per, per)
        lab_ref[here] = label
        spread_ref[here, :CH] = jnp.where(label == 1.0, inputs, 0.0).astype(BF)
        spread_ref[here, CH:] = jnp.where(label == 2.0, inputs, 0.0).astype(BF)

    def step(t, carry):
        here = pl.ds(pl.multiple_of(t * TILE, TILE), TILE)
        spread = spread_ref[here]
        factors = dot(spread, win_ref[...]).astype(BF)
        factors_ref[here] = factors
        pre = dot(factors, one_ref[...])
        pre_ref[here] = pre
        act = (pre / (1.0 + jnp.exp(-pre))).astype(BF)
        act_ref[here] = act
        lat = dot(act, two_ref[...]).astype(BF)
        lat_ref[here] = lat
        both = dot(lat, wout_ref[...])
        label = lab_ref[here]
        is0, is1 = label == 1.0, label == 2.0
        counts = jnp.where(is0, count_ref[0], jnp.where(is1, count_ref[1], 0))
        visible = iota((TILE, CH), 1) < counts
        rates = jnp.where(is0, both[:, :CH], both[:, CH:])
        rates = jnp.where(visible, rates, 0.0)
        reb_ref[here] = rates.astype(BF)
        inputs = spread[:, :CH].astype(F32) + spread[:, CH:].astype(F32)
        errors = ((rates - inputs) * weight)
        err = jnp.concatenate([jnp.where(is0, errors, 0.0), jnp.where(is1, errors, 0.0)], axis=1).astype(BF)
        err_ref[here] = err
        dlat_ref[here] = dot_cols(err, wout_ref[...]).astype(BF)
        return carry

    lax.fori_loop(0, rows // TILE, step, 0)
    core = core_ref[0]

    def grads(m, carry):
        cols = pl.ds(pl.multiple_of(m * TILE, TILE), TILE)
        gout_ref[m] = dot_rows(lat_ref[:, cols], err_ref[...]).astype(BF)
        split_pair(core, dot_rows(act_ref[:, cols], dlat_ref[...]), send_ref, own_ref, m)
        return carry

    lax.fori_loop(0, 4, grads, 0)
    for b in range(rows // per):
        slots_ref[b * wide : (b + 1) * wide] = dot_rows(pick, reb_ref[b * per : (b + 1) * per]).astype(BF)


def inner_kernel(core_ref, dlat_ref, two_ref, pre_ref, factors_ref, dpre_ref, send_ref, own_ref):
    rows = dpre_ref.shape[0]

    def step(t, carry):
        here = pl.ds(pl.multiple_of(t * TILE, TILE), TILE)
        dact = dot_cols(dlat_ref[here], two_ref[...])
        pre = pre_ref[here]
        s = 1.0 / (1.0 + jnp.exp(-pre))
        dpre_ref[here] = (dact * s * (1.0 + pre * (1.0 - s))).astype(BF)
        return carry

    lax.fori_loop(0, rows // TILE, step, 0)
    core = core_ref[0]

    def grads(m, carry):
        cols = pl.ds(pl.multiple_of(m * TILE, TILE), TILE)
        split_pair(core, dot_rows(factors_ref[:, cols], dpre_ref[...]), send_ref, own_ref, m)
        return carry

    lax.fori_loop(0, 4, grads, 0)


def readin_kernel(dpre_ref, one_ref, spread_ref, gin_ref, dfac_ref):
    rows = dpre_ref.shape[0]

    def step(t, carry):
        here = pl.ds(pl.multiple_of(t * TILE, TILE), TILE)
        dfac_ref[here] = dot_cols(dpre_ref[here], one_ref[...]).astype(BF)
        return carry

    lax.fori_loop(0, rows // TILE, step, 0)
    grad = dot_rows(spread_ref[...], dfac_ref[...]).astype(BF)
    for j in range(4):
        gin_ref[j] = grad[64 * j : 64 * j + 64]


VM = pl.BlockSpec(memory_space=pltpu.VMEM)
SM = pl.BlockSpec(memory_space=pltpu.SMEM)


def call(kernel, outs, *args, smem=0, scratch=(), flops=0, moved=0):
    return pl.pallas_call(
        kernel,
        out_shape=[jax.ShapeDtypeStruct(s, d) for s, d in outs],
        in_specs=[SM] * smem + [VM] * (len(args) - smem),
        out_specs=[VM] * len(outs),
        scratch_shapes=[pltpu.VMEM(s, d) for s, d in scratch],
        compiler_params=pltpu.CompilerParams(vmem_limit_bytes=56 * 1024 * 1024),
        cost_estimate=pl.CostEstimate(flops=flops, bytes_accessed=moved, transcendentals=0),
    )(*args)


def ring(n, k):
    return [(i, (i + k) % n) for i in range(n)]


def pick_at(x, i, axis=0):
    return lax.dynamic_index_in_dim(x, i, axis, keepdims=False)


def scatter_sum(x, axis, n):
    me = lax.axis_index(axis)
    got = [
        lax.ppermute(pick_at(x, (me + k) % n).astype(BF), axis, ring(n, k)) for k in range(1, n)
    ]
    total = pick_at(x, me).astype(F32)
    for g in got:
        total = total + g.astype(F32)
    return total


def gather(x, axis, n):
    me = lax.axis_index(axis)
    got = [x] + [lax.ppermute(x, axis, ring(n, k)) for k in range(1, n)]
    parts = []
    for j in range(n):
        part = got[0]
        for k in range(1, n):
            part = jnp.where((me - k) % n == j, got[k], part)
        parts.append(part)
    return jnp.stack(parts)


def all_sum(x, axis):
    x = x.astype(BF)
    a, b, c = [lax.ppermute(x, axis, ring(4, k)).astype(F32) for k in (1, 2, 3)]
    return (x.astype(F32) + b) + (a + c)


def layer_share(send, own):
    got = lax.ppermute(send, "core", ring(CS, 1))
    chip = own.astype(F32) + got.astype(F32)
    mine = scatter_sum(chip, "y", YS)
    parts = lax.all_to_all(mine.astype(BF), "z", split_axis=0, concat_axis=0, tiled=True)
    return jnp.sum(parts.astype(F32), axis=0)


def on_device(spikes, row_owner, row_block, chan_count, readin, readout, first_layer, second_layer):
    session = ("z", "y", "core")
    rows = spikes.shape[0]
    owners = ZS * YS * CS
    slots, count = owners * STRIDE, owners * CAP
    lat = readin.shape[1]
    core = lax.axis_index("core").astype(jnp.int32).reshape(1)
    packed, target = call(
        pack_kernel, [((slots, CH), BF), ((rows, 1), jnp.int32)], row_owner, row_block[:, None], spikes
    )
    got = lax.all_to_all(packed, session, split_axis=0, concat_axis=0, tiled=True)
    weight = (chan_count.shape[0] / rows) ** 0.5
    pair = [((YS, ZS, 16, lat), BF)] * 2
    back, gout, spread, factors, pre, dlat, send2, own2 = call(
        functools.partial(forward_kernel, weight),
        [((slots, CH), BF), ((4, TILE, TILE), BF), ((count, TILE), BF), ((count, lat), BF), ((count, lat), F32),
         ((count, lat), BF)] + pair,
        core, chan_count, got, readin, readout, first_layer, second_layer,
        smem=2,
        scratch=[((count, lat), BF), ((count, lat), BF), ((count, TILE), BF), ((count, 1), F32), ((count, CH), BF)],
        flops=7_000_000_000, moved=16_000_000,
    )
    dpre, send1, own1 = call(
        inner_kernel, [((count, lat), BF)] + pair, core, dlat, second_layer, pre, factors,
        smem=1, flops=3_200_000_000, moved=12_000_000,
    )
    (gin,) = call(
        readin_kernel, [((4, 64, lat), BF)], dpre, first_layer, spread,
        scratch=[((count, lat), BF)], flops=2_000_000_000, moved=5_000_000,
    )
    share2 = layer_share(send2, own2)
    share1 = layer_share(send1, own1)
    scale = 1.0 / (chan_count.shape[0] * owners) ** 0.5
    both = all_sum(jnp.stack([share1, share2]), "group") * scale
    out_sum = gather(scatter_sum(gout, "group", 4).astype(BF), "group", 4).astype(F32).reshape(lat, TILE)
    in_sum = gather(scatter_sum(gin, "group", 4).astype(BF), "group", 4).astype(F32).reshape(TILE, lat)
    returned = lax.all_to_all(back, session, split_axis=0, concat_axis=0, tiled=True)
    (rebuilt,) = call(unpack_kernel, [((rows, CH), BF)], target, returned)
    return rebuilt, in_sum, out_sum, both[0], both[1]


def solution(mesh):
    groups = mesh.shape["group"]
    fine = Mesh(mesh.devices.reshape(groups, ZS, YS, CS), ("group", "z", "y", "core"))
    session = ("z", "y", "core")
    rows = ("group",) + session
    return jax.shard_map(
        on_device,
        mesh=fine,
        in_specs=(P(rows, None), P(rows, None), P(rows), P(session), P(session, None), P(None, session), P(), P()),
        out_specs=(P(rows, None), P(session, None), P(None, session), P(session, None), P(session, None)),
        check_vma=False,
    )
```

```python
import functools

import jax
import jax.numpy as jnp
from jax import lax
from jax.experimental import pallas as pl
from jax.experimental.pallas import tpu as pltpu
from jax.sharding import Mesh, PartitionSpec as P

ZS, YS, CS = 8, 4, 2
CH = 128
STRIDE = 16
CAP = 12
TILE = 256
BF = jnp.bfloat16
F32 = jnp.float32
ROWS_DIMS = (((0,), (0,)), ((), ()))
COLS_DIMS = (((1,), (1,)), ((), ()))


def dot(a, b):
    return jnp.dot(a, b, preferred_element_type=F32)


def dot_rows(a, b):
    return lax.dot_general(a, b, ROWS_DIMS, preferred_element_type=F32)


def dot_cols(a, b):
    return lax.dot_general(a, b, COLS_DIMS, preferred_element_type=F32)


def iota(shape, dim):
    return lax.broadcasted_iota(jnp.int32, shape, dim)


def pack_kernel(owner_ref, block_ref, spikes_ref, packed_ref, target_ref):
    rows = spikes_ref.shape[0]
    slots = packed_ref.shape[0]
    owners = slots // STRIDE
    owner = owner_ref[...]
    match = owner == iota((owners, rows), 0)
    match_b = match.astype(F32).astype(BF)
    earlier = (iota((rows, rows), 0) < iota((rows, rows), 1)).astype(F32).astype(BF)
    before = dot(match_b, earlier)
    rank = jnp.sum(jnp.where(match, before, 0.0), axis=0, keepdims=True).astype(jnp.int32)
    target = owner * STRIDE + rank
    target_ref[...] = target
    label = (block_ref[...].reshape(1, rows) + 1).astype(F32)
    ranked = jnp.where(iota((CH, rows), 0) == rank, label, 0.0).astype(BF)
    labels = dot_cols(match_b, ranked).astype(BF)
    place = (iota((slots, rows), 0) == target).astype(F32).astype(BF)
    label_place = (iota((slots, owners), 0) == iota((slots, owners), 1) * STRIDE + CAP).astype(F32).astype(BF)
    packed_ref[...] = (dot(place, spikes_ref[...]) + dot(label_place, labels)).astype(BF)


def unpack_kernel(target_ref, back_ref, rebuilt_ref):
    rows = rebuilt_ref.shape[0]
    slots = back_ref.shape[0]
    place = (iota((slots, rows), 0) == target_ref[...]).astype(F32).astype(BF)
    rebuilt_ref[...] = dot_rows(place, back_ref[...]).astype(BF)


def split_pair(core, tile, send_ref, own_ref, at):
    cols = tile.shape[1]
    first = core == 0
    for j in range(8):
        low, high = tile[32 * j : 32 * j + 16], tile[32 * j + 16 : 32 * j + 32]
        z, y = at * 2 + j // 4, j % 4
        send_ref[y, z] = jnp.where(first, high, low).astype(BF)
        own_ref[y, z] = jnp.where(first, low, high).astype(BF)


def forward_kernel(weight, core_ref, count_ref, got_ref, win_hbm, wout_hbm, one_hbm, two_hbm,
                   slots_ref, gout_ref, spread_ref, factors_ref, slope_ref, dlat_ref, send_ref, own_ref,
                   act_ref, lat_ref, err_ref, lab_ref, reb_ref, win_ref, wout_ref, one_ref, two_ref, sems):
    weights = [
        pltpu.make_async_copy(far, near, sems.at[i])
        for i, (far, near) in enumerate(
            [(win_hbm, win_ref), (one_hbm, one_ref), (two_hbm, two_ref), (wout_hbm, wout_ref)]
        )
    ]
    for copy in weights:
        copy.start()
    rows = spread_ref.shape[0]
    per, wide = 16 * CAP, 16 * STRIDE
    row, col = iota((per, wide), 0), iota((per, wide), 1)
    source = (row * 5462) >> 16
    pick = (col == source * STRIDE + row - source * CAP).astype(F32).astype(BF)
    pick_label = (col == source * STRIDE + CAP).astype(F32).astype(BF)
    row1, lane = iota((per, CH), 0), iota((per, CH), 1)
    rank1 = row1 - ((row1 * 5462) >> 16) * CAP
    for b in range(rows // per):
        block = got_ref[b * wide : (b + 1) * wide]
        taken = dot(pick, block)
        label = jnp.sum(jnp.where(lane == rank1, dot(pick_label, block), 0.0), axis=1, keepdims=True)
        counts = jnp.where(label == 1.0, count_ref[0], jnp.where(label == 2.0, count_ref[1], 0))
        inputs = jnp.where(lane < counts, taken, 0.0)
        here = pl.ds(b * per, per)
        lab_ref[here] = label
        spread_ref[here, :CH] = jnp.where(label == 1.0, inputs, 0.0).astype(BF)
        spread_ref[here, CH:] = jnp.where(label == 2.0, inputs, 0.0).astype(BF)

    def step(t):
        here = pl.ds(t * TILE, TILE)
        spread = spread_ref[here]
        if t == 0:
            weights[0].wait()
        factors = dot(spread, win_ref[...]).astype(BF)
        factors_ref[here] = factors
        if t == 0:
            weights[1].wait()
        pre = dot(factors, one_ref[...])
        s = 0.5 * jnp.tanh(0.5 * pre) + 0.5
        silu = pre * s
        slope_ref[here] = (s + silu * (1.0 - s)).astype(BF)
        act = silu.astype(BF)
        act_ref[here] = act
        if t == 0:
            weights[2].wait()
        lat = dot(act, two_ref[...]).astype(BF)
        lat_ref[here] = lat
        if t == 0:
            weights[3].wait()
        both = dot(lat, wout_ref[...])
        label = lab_ref[here]
        is0, is1 = label == 1.0, label == 2.0
        counts = jnp.where(is0, count_ref[0], jnp.where(is1, count_ref[1], 0))
        visible = iota((TILE, CH), 1) < counts
        rates = jnp.where(is0, both[:, :CH], both[:, CH:])
        rates = jnp.where(visible, rates, 0.0)
        reb_ref[here] = rates.astype(BF)
        inputs = spread[:, :CH].astype(F32) + spread[:, CH:].astype(F32)
        errors = ((rates - inputs) * weight)
        err = jnp.concatenate([jnp.where(is0, errors, 0.0), jnp.where(is1, errors, 0.0)], axis=1).astype(BF)
        err_ref[here] = err
        dlat_ref[here] = dot_cols(err, wout_ref[...]).astype(BF)

    for t in range(rows // TILE):
        step(t)
    core = core_ref[0]

    def grads(m, carry):
        cols = pl.ds(pl.multiple_of(m * TILE, TILE), TILE)
        gout = dot_rows(lat_ref[:, cols], err_ref[...]).astype(BF)
        for q in range(4):
            gout_ref[m, :, TILE * q : TILE * q + TILE] = gout[64 * q : 64 * q + 64]
        split_pair(core, dot_rows(act_ref[:, cols], dlat_ref[...]), send_ref, own_ref, m)
        return carry

    lax.fori_loop(0, 4, grads, 0)
    for b in range(rows // per):
        slots_ref[b * wide : (b + 1) * wide] = dot_rows(pick, reb_ref[b * per : (b + 1) * per]).astype(BF)


def inner_kernel(core_ref, dlat_ref, two_ref, slope_ref, factors_ref, dpre_ref, send_ref, own_ref):
    rows = dpre_ref.shape[0]

    def step(t, carry):
        here = pl.ds(pl.multiple_of(t * TILE, TILE), TILE)
        dact = dot_cols(dlat_ref[here], two_ref[...])
        dpre_ref[here] = (dact * slope_ref[here].astype(F32)).astype(BF)
        return carry

    lax.fori_loop(0, rows // TILE, step, 0)
    core = core_ref[0]

    def grads(m, carry):
        cols = pl.ds(pl.multiple_of(m * TILE, TILE), TILE)
        split_pair(core, dot_rows(factors_ref[:, cols], dpre_ref[...]), send_ref, own_ref, m)
        return carry

    lax.fori_loop(0, 4, grads, 0)


def readin_kernel(group_ref, dpre_ref, one_ref, spread_ref, gout_ref, *refs):
    out_refs, dfac_ref, gin_ref = refs[:4], refs[4], refs[5]
    rows = dpre_ref.shape[0]
    for t in range(rows // TILE):
        here = pl.ds(t * TILE, TILE)
        dfac_ref[here] = dot_cols(dpre_ref[here], one_ref[...]).astype(BF)
    grad = dot_rows(spread_ref[...], dfac_ref[...]).astype(BF)
    for j in range(4):
        gin_ref[j] = grad[64 * j : 64 * j + 64]
    for k in range(4):
        at = lax.rem(group_ref[0] + k, 4)
        out_refs[k][:64] = gin_ref[at]
        out_refs[k][64:] = gout_ref[at]


def spread_kernel(group_ref, *refs):
    shares, in_ref, out_ref = refs[:4], refs[4], refs[5]
    for k in range(4):
        at = lax.rem(group_ref[0] + 4 - k, 4)
        in_ref[at] = shares[k][:64].astype(F32)
        for q in range(4):
            out_ref[at, 64 * q : 64 * q + 64] = shares[k][64:, TILE * q : TILE * q + TILE].astype(F32)


def pair_sum_kernel(y_ref, own_ref, got_ref, *out_refs):
    for k, out_ref in enumerate(out_refs):
        at = lax.rem(y_ref[0] + k, YS)
        out_ref[...] = (own_ref[at].astype(F32) + got_ref[at].astype(F32)).astype(BF)


def plane_sum_kernel(*refs):
    out_ref = refs[-1]
    for g in range(2):
        a, b, c, d = [r[...].astype(F32) for r in refs[4 * g : 4 * g + 4]]
        out_ref[:, 16 * g : 16 * g + 16] = ((a + b) + (c + d)).astype(BF)


VM = pl.BlockSpec(memory_space=pltpu.VMEM)
SM = pl.BlockSpec(memory_space=pltpu.SMEM)
FAR = pl.BlockSpec(memory_space=pltpu.HBM)


def call(kernel, outs, *args, smem=0, scratch=(), flops=0, moved=0, vmem=16, far=0):
    return pl.pallas_call(
        kernel,
        out_shape=[jax.ShapeDtypeStruct(s, d) for s, d in outs],
        in_specs=[SM] * smem + [VM] * (len(args) - smem - far) + [FAR] * far,
        out_specs=[VM] * len(outs),
        scratch_shapes=[pltpu.VMEM(s, d) for s, d in scratch] + ([pltpu.SemaphoreType.DMA((far,))] if far else []),
        compiler_params=pltpu.CompilerParams(vmem_limit_bytes=vmem * 1024 * 1024),
        cost_estimate=pl.CostEstimate(flops=flops, bytes_accessed=moved, transcendentals=0),
    )(*args)


def ring(n, k):
    return [(i, (i + k) % n) for i in range(n)]


def others(parts, axis):
    n = len(parts)
    return [parts[0]] + [lax.ppermute(parts[k], axis, ring(n, k)) for k in range(1, n)]


def add_all(terms):
    a, b, c, d = [t.astype(F32) for t in terms]
    return (a + c) + (b + d)


def pair_sum(own, got):
    me = lax.axis_index("y").astype(jnp.int32).reshape(1)
    shape = own.shape[1:]
    return call(pair_sum_kernel, [(shape, BF)] * YS, me, own, got, smem=1, vmem=6, moved=4_000_000)


def gather(x, axis, n):
    me = lax.axis_index(axis)
    got = [x] + [lax.ppermute(x, axis, ring(n, k)) for k in range(1, n)]
    parts = []
    for j in range(n):
        part = got[0]
        for k in range(1, n):
            part = jnp.where((me - k) % n == j, got[k], part)
        parts.append(part)
    return jnp.stack(parts)


def on_device(spikes, row_owner, row_block, chan_count, readin, readout, first_layer, second_layer):
    session = ("z", "y", "core")
    rows = spikes.shape[0]
    owners = ZS * YS * CS
    slots, count = owners * STRIDE, owners * CAP
    lat = readin.shape[1]
    core = lax.axis_index("core").astype(jnp.int32).reshape(1)
    packed, target = call(
        pack_kernel, [((slots, CH), BF), ((1, rows), jnp.int32)],
        row_owner.reshape(1, rows), row_block, spikes, vmem=60,
    )
    got = lax.all_to_all(packed, session, split_axis=0, concat_axis=0, tiled=True)
    weight = (chan_count.shape[0] / rows) ** 0.5
    pair = [((YS, ZS, 16, lat), BF)] * 2
    back, gout, spread, factors, slope, dlat, send2, own2 = call(
        functools.partial(forward_kernel, weight),
        [((slots, CH), BF), ((4, 64, lat), BF), ((count, TILE), BF), ((count, lat), BF), ((count, lat), BF),
         ((count, lat), BF)] + pair,
        core, chan_count, got, readin, readout, first_layer, second_layer,
        smem=2,
        scratch=[((count, lat), BF), ((count, lat), BF), ((count, TILE), BF), ((count, 1), F32), ((count, CH), BF),
                 (readin.shape, BF), (readout.shape, BF), (first_layer.shape, BF), (second_layer.shape, BF)],
        flops=7_000_000_000, moved=16_000_000, vmem=22, far=4,
    )
    dpre, send1, own1 = call(
        inner_kernel, [((count, lat), BF)] + pair, core, dlat, second_layer, slope, factors,
        smem=1, flops=3_200_000_000, moved=12_000_000, vmem=14,
    )
    group = lax.axis_index("group").astype(jnp.int32).reshape(1)
    parts2 = pair_sum(own2, lax.ppermute(send2, "core", ring(CS, 1)))
    parts2, dpre = lax.optimization_barrier((parts2, dpre))
    block_parts = call(
        readin_kernel, [((CH, lat), BF)] * 4, group, dpre, first_layer, spread, gout,
        scratch=[((count, lat), BF), ((4, 64, lat), BF)], smem=1, flops=2_000_000_000, moved=5_000_000, vmem=10,
    )
    terms2 = others(parts2, "y")
    parts1 = pair_sum(own1, lax.ppermute(send1, "core", ring(CS, 1)))
    parts1, block_parts, back = lax.optimization_barrier((parts1, block_parts, back))
    returned = lax.all_to_all(back, session, split_axis=0, concat_axis=0, tiled=True)
    terms1 = others(parts1, "y")
    block_terms = others(block_parts, "group")
    (mine,) = call(plane_sum_kernel, [((ZS, 32, lat), BF)], *terms1, *terms2, vmem=6, moved=6_000_000)
    mine, returned, block_terms = lax.optimization_barrier((mine, returned, block_terms))
    layer_terms = lax.all_to_all(mine, "z", split_axis=0, concat_axis=0, tiled=True)
    share = add_all(block_terms).astype(BF)
    shares = others([share] * 4, "group")
    layer_share = jnp.sum(layer_terms.astype(F32), axis=0).astype(BF)
    scale = 1.0 / (chan_count.shape[0] * owners) ** 0.5
    both = add_all(others([layer_share] * 4, "group")) * scale
    in_sum, out_sum = call(
        spread_kernel, [((4, 64, lat), F32), ((4, TILE, TILE), F32)], group, *shares, smem=1, vmem=10, moved=3_000_000
    )
    (rebuilt,) = call(unpack_kernel, [((rows, CH), BF)], target, returned, vmem=8)
    return rebuilt, in_sum.reshape(TILE, lat), out_sum.reshape(lat, TILE), both[:16], both[16:]


def solution(mesh):
    groups = mesh.shape["group"]
    fine = Mesh(mesh.devices.reshape(groups, ZS, YS, CS), ("group", "z", "y", "core"))
    session = ("z", "y", "core")
    rows = ("group",) + session
    return jax.shard_map(
        on_device,
        mesh=fine,
        in_specs=(P(rows, None), P(rows, None), P(rows), P(session), P(session, None), P(None, session), P(), P()),
        out_specs=(P(rows, None), P(session, None), P(None, session), P(session, None), P(session, None)),
        check_vma=False,
    )
```

```python
import functools

import jax
import jax.numpy as jnp
from jax import lax
from jax.experimental import pallas as pl
from jax.experimental.pallas import tpu as pltpu
from jax.sharding import Mesh, PartitionSpec as P

ZS, YS, CS = 8, 4, 2
CH = 128
STRIDE = 16
CAP = 12
TILE = 256
BF = jnp.bfloat16
F32 = jnp.float32
ROWS_DIMS = (((0,), (0,)), ((), ()))
COLS_DIMS = (((1,), (1,)), ((), ()))


def dot(a, b):
    return jnp.dot(a, b, preferred_element_type=F32)


def dot_rows(a, b):
    return lax.dot_general(a, b, ROWS_DIMS, preferred_element_type=F32)


def dot_cols(a, b):
    return lax.dot_general(a, b, COLS_DIMS, preferred_element_type=F32)


def iota(shape, dim):
    return lax.broadcasted_iota(jnp.int32, shape, dim)


def pack_kernel(owner_ref, block_ref, spikes_ref, packed_ref, target_ref):
    rows = spikes_ref.shape[0]
    slots = packed_ref.shape[0]
    owners = slots // STRIDE
    owner = owner_ref[...]
    match = owner == iota((owners, rows), 0)
    match_b = match.astype(F32).astype(BF)
    earlier = (iota((rows, rows), 0) < iota((rows, rows), 1)).astype(F32).astype(BF)
    before = dot(match_b, earlier)
    rank = jnp.sum(jnp.where(match, before, 0.0), axis=0, keepdims=True).astype(jnp.int32)
    target = owner * STRIDE + rank
    target_ref[...] = target
    label = (block_ref[...].reshape(1, rows) + 1).astype(F32)
    ranked = jnp.where(iota((CH, rows), 0) == rank, label, 0.0).astype(BF)
    labels = dot_cols(match_b, ranked).astype(BF)
    place = (iota((slots, rows), 0) == target).astype(F32).astype(BF)
    label_place = (iota((slots, owners), 0) == iota((slots, owners), 1) * STRIDE + CAP).astype(F32).astype(BF)
    packed_ref[...] = (dot(place, spikes_ref[...]) + dot(label_place, labels)).astype(BF)


def unpack_kernel(target_ref, back_ref, rebuilt_ref):
    rows = rebuilt_ref.shape[0]
    slots = back_ref.shape[0]
    place = (iota((slots, rows), 0) == target_ref[...]).astype(F32).astype(BF)
    rebuilt_ref[...] = dot_rows(place, back_ref[...]).astype(BF)


def split_pair(core, tile, send_ref, own_ref, at, layer):
    here = slice(16 * layer, 16 * layer + 16)
    first = core == 0
    for j in range(8):
        low, high = tile[32 * j : 32 * j + 16], tile[32 * j + 16 : 32 * j + 32]
        z, y = at * 2 + j // 4, j % 4
        send_ref[y, z, here] = jnp.where(first, high, low).astype(BF)
        own_ref[y, z, here] = jnp.where(first, low, high).astype(BF)


def work_kernel(weight, core_ref, group_ref, count_ref, win_hbm, one_hbm, two_hbm, wout_hbm, got_ref,
                slots_ref, part0_ref, part1_ref, part2_ref, part3_ref, send_ref, own_ref,
                win_ref, one_ref, two_ref, wout_ref, spread_ref, factors_ref, slope_ref, act_ref, lat_ref, err_ref,
                dlat_ref, lab_ref, reb_ref, gout_ref, gin_ref, sems):
    far = (win_hbm, one_hbm, two_hbm, wout_hbm)
    near = (win_ref, one_ref, two_ref, wout_ref)
    weights = [pltpu.make_async_copy(far[i], near[i], sems.at[i]) for i in range(4)]
    for copy in weights:
        copy.start()
    rows = spread_ref.shape[0]
    per, wide = 16 * CAP, 16 * STRIDE
    row, col = iota((per, wide), 0), iota((per, wide), 1)
    source = (row * 5462) >> 16
    pick = (col == source * STRIDE + row - source * CAP).astype(F32).astype(BF)
    pick_label = (col == source * STRIDE + CAP).astype(F32).astype(BF)
    row1, lane = iota((per, CH), 0), iota((per, CH), 1)
    rank1 = row1 - ((row1 * 5462) >> 16) * CAP
    for b in range(rows // per):
        block = got_ref[b * wide : (b + 1) * wide]
        taken = dot(pick, block)
        label = jnp.sum(jnp.where(lane == rank1, dot(pick_label, block), 0.0), axis=1, keepdims=True)
        counts = jnp.where(label == 1.0, count_ref[0], jnp.where(label == 2.0, count_ref[1], 0))
        inputs = jnp.where(lane < counts, taken, 0.0)
        here = pl.ds(b * per, per)
        lab_ref[here] = label
        spread_ref[here, :CH] = jnp.where(label == 1.0, inputs, 0.0).astype(BF)
        spread_ref[here, CH:] = jnp.where(label == 2.0, inputs, 0.0).astype(BF)

    def step(t):
        here = pl.ds(t * TILE, TILE)
        spread = spread_ref[here]
        if t == 0:
            weights[0].wait()
        factors = dot(spread, win_ref[...]).astype(BF)
        factors_ref[here] = factors
        if t == 0:
            weights[1].wait()
        pre = dot(factors, one_ref[...])
        s = 0.5 * jnp.tanh(0.5 * pre) + 0.5
        silu = pre * s
        slope_ref[here] = (s + silu * (1.0 - s)).astype(BF)
        act = silu.astype(BF)
        act_ref[here] = act
        if t == 0:
            weights[2].wait()
        lat = dot(act, two_ref[...]).astype(BF)
        lat_ref[here] = lat
        if t == 0:
            weights[3].wait()
        both = dot(lat, wout_ref[...])
        label = lab_ref[here]
        is0, is1 = label == 1.0, label == 2.0
        counts = jnp.where(is0, count_ref[0], jnp.where(is1, count_ref[1], 0))
        visible = iota((TILE, CH), 1) < counts
        rates = jnp.where(is0, both[:, :CH], both[:, CH:])
        rates = jnp.where(visible, rates, 0.0)
        reb_ref[here] = rates.astype(BF)
        inputs = spread[:, :CH].astype(F32) + spread[:, CH:].astype(F32)
        errors = ((rates - inputs) * weight)
        err = jnp.concatenate([jnp.where(is0, errors, 0.0), jnp.where(is1, errors, 0.0)], axis=1).astype(BF)
        err_ref[here] = err
        dlat_ref[here] = dot_cols(err, wout_ref[...]).astype(BF)

    for t in range(rows // TILE):
        step(t)
    core = core_ref[0]

    def grads(m, carry):
        cols = pl.ds(pl.multiple_of(m * TILE, TILE), TILE)
        gout = dot_rows(lat_ref[:, cols], err_ref[...]).astype(BF)
        for q in range(4):
            gout_ref[m, :, TILE * q : TILE * q + TILE] = gout[64 * q : 64 * q + 64]
        split_pair(core, dot_rows(act_ref[:, cols], dlat_ref[...]), send_ref, own_ref, m, 1)
        return carry

    lax.fori_loop(0, 4, grads, 0)
    for b in range(rows // per):
        slots_ref[b * wide : (b + 1) * wide] = dot_rows(pick, reb_ref[b * per : (b + 1) * per]).astype(BF)

    for t in range(rows // TILE):
        here = pl.ds(t * TILE, TILE)
        dact = dot_cols(dlat_ref[here], two_ref[...])
        slope_ref[here] = (dact * slope_ref[here].astype(F32)).astype(BF)

    def first(m, carry):
        cols = pl.ds(pl.multiple_of(m * TILE, TILE), TILE)
        split_pair(core, dot_rows(factors_ref[:, cols], slope_ref[...]), send_ref, own_ref, m, 0)
        return carry

    lax.fori_loop(0, 4, first, 0)
    for t in range(rows // TILE):
        here = pl.ds(t * TILE, TILE)
        dlat_ref[here] = dot_cols(slope_ref[here], one_ref[...]).astype(BF)
    grad = dot_rows(spread_ref[...], dlat_ref[...]).astype(BF)
    for j in range(4):
        gin_ref[j] = grad[64 * j : 64 * j + 64]
    for k, part_ref in enumerate((part0_ref, part1_ref, part2_ref, part3_ref)):
        at = lax.rem(group_ref[0] + k, 4)
        part_ref[:64] = gin_ref[at]
        part_ref[64:] = gout_ref[at]


def spread_kernel(group_ref, *refs):
    shares, in_ref, out_ref = refs[:4], refs[4], refs[5]
    for k in range(4):
        at = lax.rem(group_ref[0] + 4 - k, 4)
        in_ref[at] = shares[k][:64].astype(F32)
        for q in range(4):
            out_ref[at, 64 * q : 64 * q + 64] = shares[k][64:, TILE * q : TILE * q + TILE].astype(F32)


def pair_sum_kernel(y_ref, own_ref, got_ref, *out_refs):
    for k, out_ref in enumerate(out_refs):
        at = lax.rem(y_ref[0] + k, YS)
        out_ref[...] = (own_ref[at].astype(F32) + got_ref[at].astype(F32)).astype(BF)


def plane_sum_kernel(a_ref, b_ref, c_ref, d_ref, out_ref):
    a, b, c, d = [r[...].astype(F32) for r in (a_ref, b_ref, c_ref, d_ref)]
    out_ref[...] = ((a + b) + (c + d)).astype(BF)


VM = pl.BlockSpec(memory_space=pltpu.VMEM)
SM = pl.BlockSpec(memory_space=pltpu.SMEM)
ANY = pl.BlockSpec(memory_space=pl.ANY)


def call(kernel, outs, *args, smem=0, scratch=(), flops=0, moved=0, vmem=16, far=0):
    return pl.pallas_call(
        kernel,
        out_shape=[jax.ShapeDtypeStruct(s, d) for s, d in outs],
        in_specs=[SM] * smem + [ANY] * far + [VM] * (len(args) - smem - far),
        out_specs=[VM] * len(outs),
        scratch_shapes=[pltpu.VMEM(s, d) for s, d in scratch] + [pltpu.SemaphoreType.DMA((far,))] * (far > 0),
        compiler_params=pltpu.CompilerParams(vmem_limit_bytes=vmem * 1024 * 1024),
        cost_estimate=pl.CostEstimate(flops=flops, bytes_accessed=moved, transcendentals=0),
    )(*args)


def ring(n, k):
    return [(i, (i + k) % n) for i in range(n)]


def others(parts, axis):
    n = len(parts)
    return [parts[0]] + [lax.ppermute(parts[k], axis, ring(n, k)) for k in range(1, n)]


def add_all(terms):
    a, b, c, d = [t.astype(F32) for t in terms]
    return (a + c) + (b + d)


def on_device(spikes, row_owner, row_block, chan_count, readin, readout, first_layer, second_layer):
    session = ("z", "y", "core")
    rows = spikes.shape[0]
    owners = ZS * YS * CS
    slots, count = owners * STRIDE, owners * CAP
    lat = readin.shape[1]
    core = lax.axis_index("core").astype(jnp.int32).reshape(1)
    packed, target = call(
        pack_kernel, [((slots, CH), BF), ((1, rows), jnp.int32)],
        row_owner.reshape(1, rows), row_block, spikes, vmem=60,
    )
    got = lax.all_to_all(packed, session, split_axis=0, concat_axis=0, tiled=True)
    weight = (chan_count.shape[0] / rows) ** 0.5
    group = lax.axis_index("group").astype(jnp.int32).reshape(1)
    pair = ((YS, ZS, 32, lat), BF)
    tall, narrow = ((count, lat), BF), ((count, TILE), BF)
    back, *rest = call(
        functools.partial(work_kernel, weight),
        [((slots, CH), BF)] + [((CH, lat), BF)] * 4 + [pair, pair],
        core, group, chan_count, readin, first_layer, second_layer, readout, got,
        smem=3, far=4,
        scratch=[(readin.shape, BF), (first_layer.shape, BF), (second_layer.shape, BF), (readout.shape, BF),
                 narrow, tall, tall, tall, tall, narrow, tall, ((count, 1), F32), ((count, CH), BF),
                 ((4, 64, lat), BF), ((4, 64, lat), BF)],
        flops=12_000_000_000, moved=12_000_000, vmem=58,
    )
    block_parts, (send, own) = rest[:4], rest[4:]
    y_at = lax.axis_index("y").astype(jnp.int32).reshape(1)
    parts = call(
        pair_sum_kernel, [((ZS, 32, lat), BF)] * YS, y_at, own, lax.ppermute(send, "core", ring(CS, 1)),
        smem=1, vmem=10, moved=8_000_000,
    )
    parts, block_parts, back = lax.optimization_barrier((parts, block_parts, back))
    returned = lax.all_to_all(back, session, split_axis=0, concat_axis=0, tiled=True)
    block_terms = others(block_parts, "group")
    (mine,) = call(plane_sum_kernel, [((ZS, 32, lat), BF)], *others(parts, "y"), vmem=6, moved=3_000_000)
    mine, returned, block_terms = lax.optimization_barrier((mine, returned, block_terms))
    layer_terms = lax.all_to_all(mine, "z", split_axis=0, concat_axis=0, tiled=True)
    share = add_all(block_terms).astype(BF)
    shares = others([share] * 4, "group")
    layer_share = jnp.sum(layer_terms.astype(F32), axis=0).astype(BF)
    scale = 1.0 / (chan_count.shape[0] * owners) ** 0.5
    both = add_all(others([layer_share] * 4, "group")) * scale
    in_sum, out_sum = call(
        spread_kernel, [((4, 64, lat), F32), ((4, TILE, TILE), F32)], group, *shares, smem=1, vmem=10, moved=3_000_000
    )
    (rebuilt,) = call(unpack_kernel, [((rows, CH), BF)], target, returned, vmem=8)
    return rebuilt, in_sum.reshape(TILE, lat), out_sum.reshape(lat, TILE), both[:16], both[16:]


def solution(mesh):
    groups = mesh.shape["group"]
    fine = Mesh(mesh.devices.reshape(groups, ZS, YS, CS), ("group", "z", "y", "core"))
    session = ("z", "y", "core")
    rows = ("group",) + session
    return jax.shard_map(
        on_device,
        mesh=fine,
        in_specs=(P(rows, None), P(rows, None), P(rows), P(session), P(session, None), P(None, session), P(), P()),
        out_specs=(P(rows, None), P(session, None), P(None, session), P(session, None), P(session, None)),
        check_vma=False,
    )
```

```python
import functools

import jax
import jax.numpy as jnp
from jax import lax
from jax.experimental import pallas as pl
from jax.experimental.pallas import tpu as pltpu
from jax.sharding import Mesh, PartitionSpec as P

ZS, YS, CS = 8, 4, 2
CH = 128
STRIDE = 16
CAP = 12
TILE = 256
BF = jnp.bfloat16
F32 = jnp.float32
ROWS_DIMS = (((0,), (0,)), ((), ()))
COLS_DIMS = (((1,), (1,)), ((), ()))


def dot(a, b):
    return jnp.dot(a, b, preferred_element_type=F32)


def dot_rows(a, b):
    return lax.dot_general(a, b, ROWS_DIMS, preferred_element_type=F32)


def dot_cols(a, b):
    return lax.dot_general(a, b, COLS_DIMS, preferred_element_type=F32)


def iota(shape, dim):
    return lax.broadcasted_iota(jnp.int32, shape, dim)


def pack_kernel(owner_ref, block_ref, spikes_ref, packed_ref, target_ref):
    rows = spikes_ref.shape[0]
    slots = packed_ref.shape[0]
    owners = slots // STRIDE
    owner = owner_ref[...]
    match = owner == iota((owners, rows), 0)
    match_b = match.astype(F32).astype(BF)
    earlier = (iota((rows, rows), 0) < iota((rows, rows), 1)).astype(F32).astype(BF)
    before = dot(match_b, earlier)
    rank = jnp.sum(jnp.where(match, before, 0.0), axis=0, keepdims=True).astype(jnp.int32)
    target = owner * STRIDE + rank
    target_ref[...] = target
    label = (block_ref[...].reshape(1, rows) + 1).astype(F32)
    ranked = jnp.where(iota((CH, rows), 0) == rank, label, 0.0).astype(BF)
    labels = dot_cols(match_b, ranked).astype(BF)
    place = (iota((slots, rows), 0) == target).astype(F32).astype(BF)
    label_place = (iota((slots, owners), 0) == iota((slots, owners), 1) * STRIDE + CAP).astype(F32).astype(BF)
    packed_ref[...] = (dot(place, spikes_ref[...]) + dot(label_place, labels)).astype(BF)


def unpack_kernel(target_ref, back_ref, rebuilt_ref):
    rows = rebuilt_ref.shape[0]
    slots = back_ref.shape[0]
    place = (iota((slots, rows), 0) == target_ref[...]).astype(F32).astype(BF)
    rebuilt_ref[...] = dot_rows(place, back_ref[...]).astype(BF)


def split_pair(core, tile, send_ref, own_ref, at, layer):
    here = slice(16 * layer, 16 * layer + 16)
    first = core == 0
    for j in range(8):
        low, high = tile[32 * j : 32 * j + 16], tile[32 * j + 16 : 32 * j + 32]
        z, y = at * 2 + j // 4, j % 4
        send_ref[y, z, here] = jnp.where(first, high, low).astype(BF)
        own_ref[y, z, here] = jnp.where(first, low, high).astype(BF)


def work_kernel(weight, core_ref, group_ref, count_ref, win_hbm, one_hbm, two_hbm, wout_hbm, got_ref,
                slots_ref, part0_ref, part1_ref, part2_ref, part3_ref, send_ref, own_ref,
                win_ref, one_ref, two_ref, wout_ref, spread_ref, factors_ref, slope_ref, act_ref, lat_ref, err_ref,
                dlat_ref, lab_ref, reb_ref, gout_ref, gin_ref, sems):
    far = (win_hbm, one_hbm, two_hbm, wout_hbm)
    near = (win_ref, one_ref, two_ref, wout_ref)
    weights = [pltpu.make_async_copy(far[i], near[i], sems.at[i]) for i in range(4)]
    for copy in weights:
        copy.start()
    rows = spread_ref.shape[0]
    per, wide = 16 * CAP, 16 * STRIDE
    row, col = iota((per, wide), 0), iota((per, wide), 1)
    source = (row * 5462) >> 16
    pick = (col == source * STRIDE + row - source * CAP).astype(F32).astype(BF)
    pick_label = (col == source * STRIDE + CAP).astype(F32).astype(BF)
    row1, lane = iota((per, CH), 0), iota((per, CH), 1)
    rank1 = row1 - ((row1 * 5462) >> 16) * CAP
    for b in range(rows // per):
        block = got_ref[b * wide : (b + 1) * wide]
        taken = dot(pick, block)
        label = jnp.sum(jnp.where(lane == rank1, dot(pick_label, block), 0.0), axis=1, keepdims=True)
        counts = jnp.where(label == 1.0, count_ref[0], jnp.where(label == 2.0, count_ref[1], 0))
        inputs = jnp.where(lane < counts, taken, 0.0)
        here = pl.ds(b * per, per)
        lab_ref[here] = label
        spread_ref[here, :CH] = jnp.where(label == 1.0, inputs, 0.0).astype(BF)
        spread_ref[here, CH:] = jnp.where(label == 2.0, inputs, 0.0).astype(BF)

    def step(t):
        here = pl.ds(t * TILE, TILE)
        spread = spread_ref[here]
        if t == 0:
            weights[0].wait()
        factors = dot(spread, win_ref[...]).astype(BF)
        factors_ref[here] = factors
        if t == 0:
            weights[1].wait()
        pre = dot(factors, one_ref[...])
        s = 0.5 * jnp.tanh(0.5 * pre) + 0.5
        silu = pre * s
        slope_ref[here] = (s + silu * (1.0 - s)).astype(BF)
        act = silu.astype(BF)
        act_ref[here] = act
        if t == 0:
            weights[2].wait()
        lat = dot(act, two_ref[...]).astype(BF)
        lat_ref[here] = lat
        if t == 0:
            weights[3].wait()
        both = dot(lat, wout_ref[...])
        label = lab_ref[here]
        is0, is1 = label == 1.0, label == 2.0
        counts = jnp.where(is0, count_ref[0], jnp.where(is1, count_ref[1], 0))
        visible = iota((TILE, CH), 1) < counts
        rates = jnp.where(is0, both[:, :CH], both[:, CH:])
        rates = jnp.where(visible, rates, 0.0)
        reb_ref[here] = rates.astype(BF)
        inputs = spread[:, :CH].astype(F32) + spread[:, CH:].astype(F32)
        errors = ((rates - inputs) * weight)
        err = jnp.concatenate([jnp.where(is0, errors, 0.0), jnp.where(is1, errors, 0.0)], axis=1).astype(BF)
        err_ref[here] = err
        dlat_ref[here] = dot_cols(err, wout_ref[...]).astype(BF)

    for t in range(rows // TILE):
        step(t)
    core = core_ref[0]

    def grads(m, carry):
        cols = pl.ds(pl.multiple_of(m * TILE, TILE), TILE)
        gout = dot_rows(lat_ref[:, cols], err_ref[...]).astype(BF)
        for q in range(4):
            gout_ref[m, :, TILE * q : TILE * q + TILE] = gout[64 * q : 64 * q + 64]
        split_pair(core, dot_rows(act_ref[:, cols], dlat_ref[...]), send_ref, own_ref, m, 1)
        return carry

    lax.fori_loop(0, 4, grads, 0)
    for b in range(rows // per):
        slots_ref[b * wide : (b + 1) * wide] = dot_rows(pick, reb_ref[b * per : (b + 1) * per]).astype(BF)

    for t in range(rows // TILE):
        here = pl.ds(t * TILE, TILE)
        dact = dot_cols(dlat_ref[here], two_ref[...])
        slope_ref[here] = (dact * slope_ref[here].astype(F32)).astype(BF)

    def first(m, carry):
        cols = pl.ds(pl.multiple_of(m * TILE, TILE), TILE)
        split_pair(core, dot_rows(factors_ref[:, cols], slope_ref[...]), send_ref, own_ref, m, 0)
        return carry

    lax.fori_loop(0, 4, first, 0)
    for t in range(rows // TILE):
        here = pl.ds(t * TILE, TILE)
        dlat_ref[here] = dot_cols(slope_ref[here], one_ref[...]).astype(BF)
    grad = dot_rows(spread_ref[...], dlat_ref[...]).astype(BF)
    for j in range(4):
        gin_ref[j] = grad[64 * j : 64 * j + 64]
    for k, part_ref in enumerate((part0_ref, part1_ref, part2_ref, part3_ref)):
        at = lax.rem(group_ref[0] + k, 4)
        part_ref[:64] = gin_ref[at]
        part_ref[64:] = gout_ref[at]


def spread_kernel(group_ref, *refs):
    shares, in_ref, out_ref = refs[:4], refs[4], refs[5]
    for k in range(4):
        at = lax.rem(group_ref[0] + 4 - k, 4)
        in_ref[at] = shares[k][:64].astype(F32)
        for q in range(4):
            out_ref[at, 64 * q : 64 * q + 64] = shares[k][64:, TILE * q : TILE * q + TILE].astype(F32)


def pair_sum_kernel(y_ref, own_ref, got_ref, mine_ref, *out_refs):
    for k in range(YS):
        at = lax.rem(y_ref[0] + k, YS)
        total = (own_ref[at].astype(F32) + got_ref[at].astype(F32)).astype(BF)
        if k == 0:
            mine_ref[...] = total
        else:
            out_refs[2 * k - 2][...] = total[:, :16]
            out_refs[2 * k - 1][...] = total[:, 16:]


def relay_kernel(up_ref, got_up_ref, down_ref, got_down_ref, up_out_ref, down_out_ref):
    up_out_ref[...] = (up_ref[...].astype(F32) + got_up_ref[...].astype(F32)).astype(BF)
    down_out_ref[...] = (down_ref[...].astype(F32) + got_down_ref[...].astype(F32)).astype(BF)


def plane_sum_kernel(mine_ref, up1_ref, down1_ref, up2_ref, down2_ref, out_ref):
    for at, up_ref, down_ref in ((0, up1_ref, down1_ref), (16, up2_ref, down2_ref)):
        mine = mine_ref[:, at : at + 16].astype(F32)
        out_ref[:, at : at + 16] = (mine + (up_ref[...].astype(F32) + down_ref[...].astype(F32))).astype(BF)


VM = pl.BlockSpec(memory_space=pltpu.VMEM)
SM = pl.BlockSpec(memory_space=pltpu.SMEM)
ANY = pl.BlockSpec(memory_space=pl.ANY)


def call(kernel, outs, *args, smem=0, scratch=(), flops=0, moved=0, vmem=16, far=0):
    return pl.pallas_call(
        kernel,
        out_shape=[jax.ShapeDtypeStruct(s, d) for s, d in outs],
        in_specs=[SM] * smem + [ANY] * far + [VM] * (len(args) - smem - far),
        out_specs=[VM] * len(outs),
        scratch_shapes=[pltpu.VMEM(s, d) for s, d in scratch] + [pltpu.SemaphoreType.DMA((far,))] * (far > 0),
        compiler_params=pltpu.CompilerParams(vmem_limit_bytes=vmem * 1024 * 1024),
        cost_estimate=pl.CostEstimate(flops=flops, bytes_accessed=moved, transcendentals=0),
    )(*args)


def ring(n, k):
    return [(i, (i + k) % n) for i in range(n)]


def others(parts, axis):
    n = len(parts)
    return [parts[0]] + [lax.ppermute(parts[k], axis, ring(n, k)) for k in range(1, n)]


def add_all(terms):
    a, b, c, d = [t.astype(F32) for t in terms]
    return (a + c) + (b + d)


def on_device(spikes, row_owner, row_block, chan_count, readin, readout, first_layer, second_layer):
    session = ("z", "y", "core")
    rows = spikes.shape[0]
    owners = ZS * YS * CS
    slots, count = owners * STRIDE, owners * CAP
    lat = readin.shape[1]
    core = lax.axis_index("core").astype(jnp.int32).reshape(1)
    packed, target = call(
        pack_kernel, [((slots, CH), BF), ((1, rows), jnp.int32)],
        row_owner.reshape(1, rows), row_block, spikes, vmem=60,
    )
    got = lax.all_to_all(packed, session, split_axis=0, concat_axis=0, tiled=True)
    weight = (chan_count.shape[0] / rows) ** 0.5
    group = lax.axis_index("group").astype(jnp.int32).reshape(1)
    pair = ((YS, ZS, 32, lat), BF)
    tall, narrow = ((count, lat), BF), ((count, TILE), BF)
    back, *rest = call(
        functools.partial(work_kernel, weight),
        [((slots, CH), BF)] + [((CH, lat), BF)] * 4 + [pair, pair],
        core, group, chan_count, readin, first_layer, second_layer, readout, got,
        smem=3, far=4,
        scratch=[(readin.shape, BF), (first_layer.shape, BF), (second_layer.shape, BF), (readout.shape, BF),
                 narrow, tall, tall, tall, tall, narrow, tall, ((count, 1), F32), ((count, CH), BF),
                 ((4, 64, lat), BF), ((4, 64, lat), BF)],
        flops=12_000_000_000, moved=12_000_000, vmem=58,
    )
    block_parts, (send, own) = rest[:4], rest[4:]
    y_at = lax.axis_index("y").astype(jnp.int32).reshape(1)
    chunk = ((ZS, 16, lat), BF)
    parts = call(
        pair_sum_kernel, [((ZS, 32, lat), BF)] + [chunk] * 6, y_at, own, lax.ppermute(send, "core", ring(CS, 1)),
        smem=1, vmem=10, moved=8_000_000,
    )
    parts, block_parts, back = lax.optimization_barrier((parts, block_parts, back))
    returned = lax.all_to_all(back, session, split_axis=0, concat_axis=0, tiled=True)
    block_terms = others(block_parts, "group")
    mine, next1, next2, two1, two2, last1, last2 = parts
    up, down = ring(YS, 1), ring(YS, YS - 1)
    got_up, got_down = lax.ppermute(two1, "y", up), lax.ppermute(two2, "y", down)
    up2, down1 = lax.ppermute(next2, "y", up), lax.ppermute(last1, "y", down)
    relay_up, relay_down = call(relay_kernel, [chunk] * 2, next1, got_up, last2, got_down, vmem=6, moved=2_000_000)
    up1, down2 = lax.ppermute(relay_up, "y", up), lax.ppermute(relay_down, "y", down)
    (mine,) = call(
        plane_sum_kernel, [((ZS, 32, lat), BF)], mine, up1, down1, up2, down2, vmem=6, moved=3_000_000
    )
    mine, returned, block_terms = lax.optimization_barrier((mine, returned, block_terms))
    layer_terms = lax.all_to_all(mine, "z", split_axis=0, concat_axis=0, tiled=True)
    share = add_all(block_terms).astype(BF)
    shares = others([share] * 4, "group")
    layer_share = jnp.sum(layer_terms.astype(F32), axis=0).astype(BF)
    scale = 1.0 / (chan_count.shape[0] * owners) ** 0.5
    both = add_all(others([layer_share] * 4, "group")) * scale
    in_sum, out_sum = call(
        spread_kernel, [((4, 64, lat), F32), ((4, TILE, TILE), F32)], group, *shares, smem=1, vmem=10, moved=3_000_000
    )
    (rebuilt,) = call(unpack_kernel, [((rows, CH), BF)], target, returned, vmem=8)
    return rebuilt, in_sum.reshape(TILE, lat), out_sum.reshape(lat, TILE), both[:16], both[16:]


def solution(mesh):
    groups = mesh.shape["group"]
    fine = Mesh(mesh.devices.reshape(groups, ZS, YS, CS), ("group", "z", "y", "core"))
    session = ("z", "y", "core")
    rows = ("group",) + session
    return jax.shard_map(
        on_device,
        mesh=fine,
        in_specs=(P(rows, None), P(rows, None), P(rows), P(session), P(session, None), P(None, session), P(), P()),
        out_specs=(P(rows, None), P(session, None), P(None, session), P(session, None), P(session, None)),
        check_vma=False,
    )
```
